32 devices in a mesh: span: 4 (over y, x), tm: 8 (over z, core).
Axes of the slice: x: 2, y: 2, z: 4, core: 2. Of those that a mesh axis runs over, the one named last changes fastest.
Arguments:
- launched: float32 [8, 2, 110, 2048], P(None, None, None, 'tm'), may hold values from -1.5 to 1.5
- coupling: float32 [4, 2, 2, 2, 110, 110], P('span'), may hold values from -2 to 2
- impulse: float32 [4, 2, 2, 2, 129], P('span'), may hold values from -1.5 to 1.5
- amplifier: float32 [4, 2, 110], P('span'), may hold values from 0.9 to 1.11
- nonlinear: float32 [4, 2, 2], P('span'), may hold values from 0.002 to 0.008
Outputs:
- monitored: float32 [4, 8, 2, 110, 2048], P('span', None, None, None, 'tm')
The draws below stay inside these ranges and needn't reach their ends.
All inputs are finite; a program needn't handle non-finite values.
Results may differ from the reference program's by a relative error of at most 0.0004.
Values sent between devices are 32-bit elements; how exact they have to be, the bound alone decides.
A program may use at most 64 MiB of HBM per device.

```python
import math
import jax
import jax.numpy as jnp
from jax import lax

CH = 110
HALF = 64
STEPS = 2
SPANS = 2
SAMP = 256
FRAMES = 8
GROUPS = 4
N_SPAN = 4
N_TM = 8


def noise_field(key, shape, deviation):
    return deviation * jnp.clip(jax.random.normal(key, shape, jnp.float32), -3.0, 3.0)


def draw_launched(key, part):
    shape = (FRAMES, 2, CH, SAMP * N_TM)
    return noise_field(key, shape, 0.5)


def draw_coupling(key, part):
    shape = (N_SPAN, SPANS, STEPS, 2, CH, CH)
    deviation = 0.5 / (2.0 * CH) ** 0.5
    noise = noise_field(key, shape, deviation)
    identity = jnp.eye(CH, dtype=jnp.float32)
    component = (jnp.arange(2) == 0).astype(jnp.float32)
    return noise + 0.85 * component[:, None, None] * identity[None, :, :]


def draw_impulse(key, part):
    taps = 2 * HALF + 1
    shape = (N_SPAN, SPANS, STEPS, 2, taps)
    deviation = 0.6 / (2.0 * taps) ** 0.5
    noise = noise_field(key, shape, deviation)
    centre = (jnp.arange(taps) == HALF).astype(jnp.float32)
    component = (jnp.arange(2) == 0).astype(jnp.float32)
    return noise + 0.8 * component[:, None] * centre[None, :]


def draw_amplifier(key, part):
    shape = (N_SPAN, SPANS, CH)
    exponent = jnp.clip(0.05 * jax.random.normal(key, shape, jnp.float32), -0.1, 0.1)
    return jnp.exp(exponent)


def block_scale(stream_key, extent, split, least, high):
    gain = 1.0
    for dim, shards_of in split:
        steps = jax.random.uniform(jax.random.fold_in(jax.random.fold_in(stream_key, 6), dim), (shards_of,), jnp.float32, least / len(split), high / len(split))
        gain = gain * jnp.repeat(jnp.exp(steps), extent[dim] // shards_of).reshape((-1,) + (1,) * (len(extent) - 1 - dim))
    return gain


def setup_inputs(seed: int = 0) -> dict:
    key_list = jax.random.split(jax.random.key(seed), 6)
    return {
        "launched": draw_launched(jax.random.fold_in(key_list[5], 71), 0),
        "coupling": draw_coupling(jax.random.fold_in(key_list[5], 71), 0),
        "impulse": draw_impulse(jax.random.fold_in(key_list[5], 71), 0),
        "amplifier": draw_amplifier(jax.random.fold_in(key_list[5], 71), 0),
        "nonlinear": jnp.clip(jnp.exp(math.log(0.008) - 1.3862944 * jax.random.uniform(key_list[4], (GROUPS, SPANS, STEPS), jnp.float32) ** block_scale(key_list[4], (GROUPS, SPANS, STEPS), ((0, 4),), -0.2, 0.2)), 0.002, 0.008),
    }


def split_step(signal, coupling_step, impulse_step, nonlinear_step):
    length = signal.shape[-1]
    total = length + 2 * HALF
    samples = signal[:, 0] + 1j * signal[:, 1]
    padded = jnp.pad(samples, ((0, 0), (0, 0), (HALF, HALF)))
    response = impulse_step[0] + 1j * impulse_step[1]
    kernel = jnp.concatenate([response[:1], jnp.zeros((total - 2 * HALF - 1,), response.dtype), response[:0:-1]])
    spectrum = jnp.fft.fft(padded, axis=-1) * jnp.fft.fft(kernel)[None, None, :]
    result = jnp.fft.ifft(spectrum, axis=-1)[..., :length]
    real_in = jnp.real(result)
    imag_in = jnp.imag(result)
    highest = lax.Precision.HIGHEST
    real_mat = coupling_step[0]
    imag_mat = coupling_step[1]
    real_out = jnp.einsum("cd,fdt->fct", real_mat, real_in, precision=highest) - jnp.einsum("cd,fdt->fct", imag_mat, imag_in, precision=highest)
    imag_out = jnp.einsum("cd,fdt->fct", imag_mat, real_in, precision=highest) + jnp.einsum("cd,fdt->fct", real_mat, imag_in, precision=highest)
    power = jnp.sum(real_out * real_out + imag_out * imag_out, axis=1, keepdims=True)
    phase = nonlinear_step * power
    cosine = jnp.cos(phase)
    sine = jnp.sin(phase)
    return jnp.stack([real_out * cosine - imag_out * sine, real_out * sine + imag_out * cosine], axis=1)


def reference(launched, coupling, impulse, amplifier, nonlinear):
    signal = launched
    outputs = []
    for group in range(GROUPS):
        for span_index in range(SPANS):
            for step_index in range(STEPS):
                signal = split_step(signal, coupling[group, span_index, step_index], impulse[group, span_index, step_index], nonlinear[group, span_index, step_index])
            signal = signal * amplifier[group, span_index][None, None, :, None]
        outputs.append(signal)
    return jnp.stack(outputs)
```

```python
import functools

import jax
import jax.numpy as jnp
from jax import lax
from jax.experimental import pallas as pl
from jax.experimental.pallas import tpu as pltpu
from jax.sharding import PartitionSpec as P

MESH = pl.DeviceIdType.MESH
LANES = 128


def padded_rows(channels):
    return (channels + 15) // 16 * 16


def halves(value):
    high = value.astype(jnp.bfloat16)
    low = (value - high.astype(jnp.float32)).astype(jnp.bfloat16)
    return high, low


def product(a_high, a_low, b_high, b_low):
    def dot(a, b):
        return jnp.dot(a, b, preferred_element_type=jnp.float32)

    return dot(a_high, b_high) + dot(a_low, b_high) + dot(a_high, b_low)


def cos_sin(angle):
    turns = jnp.floor(angle * 0.6366197723675814 + 0.5)
    r = angle - turns * 1.5703125
    r = r - turns * 4.837512969970703e-4
    r = r - turns * 7.549789948768648e-8
    z = r * r
    sine = r + r * z * (-1.6666654611e-1 + z * (8.3321608736e-3 - z * 1.9515295891e-4))
    cosine = 1.0 - 0.5 * z + z * z * (
        4.166664568298827e-2 + z * (-1.388731625493765e-3 + z * 2.443315711809948e-5)
    )
    quadrant = turns - 4.0 * jnp.floor(turns * 0.25)
    odd = (quadrant == 1.0) | (quadrant == 3.0)
    cos_sign = jnp.where((quadrant == 1.0) | (quadrant == 2.0), -1.0, 1.0)
    sin_sign = jnp.where(quadrant >= 2.0, -1.0, 1.0)
    return cos_sign * jnp.where(odd, sine, cosine), sin_sign * jnp.where(odd, cosine, sine)


def kernel(
    sizes,
    launched_ref,
    pack_ref,
    out_ref,
    lstage,
    own,
    low_halo,
    high_halo,
    packs,
    mix_high,
    mix_low,
    fir_high,
    fir_low,
    ostage,
    lsem,
    psem,
    pack_send,
    pack_recv,
    up_send,
    up_recv,
    down_send,
    down_recv,
    out_send,
    out_recv,
):
    n_span, n_tm, spans, steps, channels, samples, per, edge = sizes
    rows = padded_rows(channels)
    rounds = n_span * spans
    me = lax.axis_index("span")
    tm = lax.axis_index("tm")
    above = jnp.minimum(tm + 1, n_tm - 1)
    below = jnp.maximum(tm - 1, 0)
    has_below = tm > 0
    has_above = tm < n_tm - 1

    def load(f):
        return pltpu.make_async_copy(launched_ref.at[me * per + f], lstage.at[f], lsem.at[f])

    def own_pack(r):
        return pltpu.make_async_copy(pack_ref.at[r], packs.at[me, r], psem.at[r])

    def give_pack(r, by):
        return pltpu.make_async_remote_copy(
            src_ref=pack_ref.at[r],
            dst_ref=packs.at[me, r],
            send_sem=pack_send.at[r, by],
            recv_sem=pack_recv.at[me, r],
            device_id={"span": lax.rem(me + by, n_span)},
            device_id_type=MESH,
        )

    def got_pack(g, r):
        return pltpu.make_async_remote_copy(
            src_ref=pack_ref.at[r],
            dst_ref=packs.at[g, r],
            send_sem=pack_send.at[r, 1],
            recv_sem=pack_recv.at[g, r],
            device_id={"span": g},
            device_id_type=MESH,
        )

    def go_up(t, f):
        return pltpu.make_async_remote_copy(
            src_ref=own.at[t, f, :, pl.ds(samples - edge, edge)],
            dst_ref=low_halo.at[t, f],
            send_sem=up_send.at[t, f],
            recv_sem=up_recv.at[t, f],
            device_id={"tm": above},
            device_id_type=MESH,
        )

    def go_down(t, f):
        return pltpu.make_async_remote_copy(
            src_ref=own.at[t, f, :, pl.ds(0, edge)],
            dst_ref=high_halo.at[t, f],
            send_sem=down_send.at[t, f],
            recv_sem=down_recv.at[t, f],
            device_id={"tm": below},
            device_id_type=MESH,
        )

    def send_edges(t, f):
        @pl.when(has_above)
        def _():
            go_up(t, f).start()

        @pl.when(has_below)
        def _():
            go_down(t, f).start()

    def keep_out(g, f):
        return pltpu.make_async_copy(
            ostage.at[g, f], out_ref.at[0, me * per + f], out_send.at[g, f]
        )

    def send_out(g, f):
        return pltpu.make_async_remote_copy(
            src_ref=ostage.at[g, f],
            dst_ref=out_ref.at[0, me * per + f],
            send_sem=out_send.at[g, f],
            recv_sem=out_recv.at[me, f],
            device_id={"span": g},
            device_id_type=MESH,
        )

    def got_out(source, f):
        return pltpu.make_async_remote_copy(
            src_ref=ostage.at[0, f],
            dst_ref=out_ref.at[0, source * per + f],
            send_sem=out_send.at[0, f],
            recv_sem=out_recv.at[source, f],
            device_id={"span": source},
            device_id_type=MESH,
        )

    for f in range(per):
        load(f).start()
    for r in range(spans):
        own_pack(r).start()

    barrier = pltpu.get_barrier_semaphore()
    for by in range(1, n_span):
        pl.semaphore_signal(
            barrier, inc=1, device_id={"span": lax.rem(me + by, n_span)}, device_id_type=MESH
        )

    @pl.when(has_above)
    def _():
        pl.semaphore_signal(barrier, inc=1, device_id={"tm": above}, device_id_type=MESH)

    @pl.when(has_below)
    def _():
        pl.semaphore_signal(barrier, inc=1, device_id={"tm": below}, device_id_type=MESH)

    for f in range(per):
        load(f).wait()
        for part in range(2):
            own[0, f, pl.ds(part * rows + rows - 8, 8), :] = jnp.zeros((8, samples), jnp.float32)
            own[0, f, pl.ds(part * rows, channels), :] = lstage[f, part]

    pl.semaphore_wait(
        barrier,
        n_span - 1 + jnp.where(has_above, 1, 0) + jnp.where(has_below, 1, 0),
    )
    for r in range(spans):
        for by in range(1, n_span):
            give_pack(r, by).start()
        if r == 0:
            for f in range(per):
                send_edges(0, f)
    for r in range(spans):
        own_pack(r).wait()

    def prepare(t):
        g = t // spans
        r = t % spans

        @pl.when(g != me)
        def _():
            got_pack(g, r).wait_recv()

        for k in range(steps):
            pack = packs[g, r, k]
            real = pack[:rows, :LANES]
            imag = pack[:rows, LANES:]
            mixer = jnp.concatenate(
                [
                    jnp.concatenate([real, -imag], axis=1),
                    jnp.concatenate([imag, real], axis=1),
                ],
                axis=0,
            )
            mix_high[k], mix_low[k] = halves(mixer)
            for part in range(2):
                line = jnp.broadcast_to(pack[rows + part : rows + part + 1], (LANES, 2 * LANES))
                band = pltpu.roll(line, 0, 1, stride=1, stride_axis=0)
                column = pl.ds(part * LANES, LANES)
                high, low = halves(band)
                fir_high[k, pl.ds(0, LANES), column] = high[:, :LANES]
                fir_high[k, pl.ds(LANES, LANES), column] = high[:, LANES:]
                fir_low[k, pl.ds(0, LANES), column] = low[:, :LANES]
                fir_low[k, pl.ds(LANES, LANES), column] = low[:, LANES:]

    gap = jnp.zeros((LANES - rows, 1), jnp.bfloat16)

    def spread(real, imag):
        fill = jnp.broadcast_to(gap, (LANES - rows, real.shape[1]))
        return jnp.concatenate([real, fill, imag, fill], axis=0)

    def advance(t, f):
        g = t // spans
        r = t % spans
        blocks = (
            [low_halo[t, f, :, pl.ds(i, LANES)] for i in range(0, edge, LANES)]
            + [own[t, f, :, pl.ds(i, LANES)] for i in range(0, samples, LANES)]
            + [high_halo[t, f, :, pl.ds(i, LANES)] for i in range(0, edge, LANES)]
        )
        margin = edge
        for k in range(steps):
            margin = margin - edge // steps
            split = [halves(block) for block in blocks]
            count = len(blocks) - 1
            high = jnp.concatenate(
                [
                    jnp.concatenate([split[b][0], split[b + 1][0]], axis=1)
                    for b in range(count)
                ],
                axis=0,
            )
            low = jnp.concatenate(
                [
                    jnp.concatenate([split[b][1], split[b + 1][1]], axis=1)
                    for b in range(count)
                ],
                axis=0,
            )
            wide = product(high, low, fir_high[k], fir_low[k])
            real_parts = []
            imag_parts = []
            for b in range(count):
                top = wide[b * 2 * rows : b * 2 * rows + rows]
                bottom = wide[b * 2 * rows + rows : (b + 1) * 2 * rows]
                real_parts.append(top[:, :LANES] - bottom[:, LANES:])
                imag_parts.append(top[:, LANES:] + bottom[:, :LANES])
            real = jnp.concatenate(real_parts, axis=1)
            imag = jnp.concatenate(imag_parts, axis=1)
            if margin > 0:
                extent = count * LANES
                place = tm * samples - margin + lax.broadcasted_iota(jnp.int32, (1, extent), 1)
                inside = ((place >= 0) & (place < samples * n_tm)).astype(jnp.float32)
                real = real * inside
                imag = imag * inside
            real_high, real_low = halves(real)
            imag_high, imag_low = halves(imag)
            mixed = product(
                mix_high[k],
                mix_low[k],
                spread(real_high, imag_high),
                spread(real_low, imag_low),
            )
            power = jnp.sum(mixed * mixed, axis=0, keepdims=True)
            cosine, sine = cos_sin(power * packs[g, r, k, 0:1, LANES - 2 : LANES - 1])
            real = mixed[:rows] * cosine - mixed[rows:] * sine
            imag = mixed[:rows] * sine + mixed[rows:] * cosine
            if k == steps - 1:
                gain = packs[g, r, k, :rows, LANES - 1 : LANES]
                real = real * gain
                imag = imag * gain
            both = jnp.concatenate([real, imag], axis=0)
            blocks = [both[:, b * LANES : (b + 1) * LANES] for b in range(count)]
        own[t + 1, f] = both

        @pl.when(t + 1 < rounds)
        def _():
            send_edges(t + 1, f)

        @pl.when(r == spans - 1)
        def _():
            ostage[g, f, 0] = real[:channels]
            ostage[g, f, 1] = imag[:channels]

            @pl.when(g == me)
            def _():
                keep_out(g, f).start()

            @pl.when(g != me)
            def _():
                send_out(g, f).start()

    prepare(0)

    def one_round(t, carry):
        for f in range(per):

            @pl.when(has_below)
            def _():
                go_up(t, f).wait_recv()

            @pl.when(jnp.logical_not(has_below))
            def _():
                low_halo[t, f] = jnp.zeros(low_halo.shape[2:], jnp.float32)

            @pl.when(has_above)
            def _():
                go_down(t, f).wait_recv()

            @pl.when(jnp.logical_not(has_above))
            def _():
                high_halo[t, f] = jnp.zeros(high_halo.shape[2:], jnp.float32)

            advance(t, f)

        @pl.when(t + 1 < rounds)
        def _():
            prepare(t + 1)

        return carry

    lax.fori_loop(0, rounds, one_round, 0)

    def drain(t, carry):
        for f in range(per):

            @pl.when(has_above)
            def _():
                go_up(t, f).wait_send()

            @pl.when(has_below)
            def _():
                go_down(t, f).wait_send()

        return carry

    lax.fori_loop(0, rounds, drain, 0)
    for r in range(spans):
        for by in range(1, n_span):
            give_pack(r, by).wait_send()

    def finish(g, carry):
        for f in range(per):

            @pl.when(g == me)
            def _():
                keep_out(g, f).wait()

            @pl.when(g != me)
            def _():
                send_out(g, f).wait_send()
                got_out(g, f).wait_recv()

        return carry

    lax.fori_loop(0, n_span, finish, 0)


def packed(coupling, impulse, amplifier, nonlinear):
    spans, steps, _, channels, _ = coupling.shape
    rows = padded_rows(channels)
    taps = impulse.shape[-1]
    gains = jnp.broadcast_to(amplifier[:, None, :, None], (spans, steps, channels, 1))
    rates = jnp.broadcast_to(nonlinear[:, :, None, None], (spans, steps, channels, 1))
    gap = jnp.zeros((spans, steps, channels, LANES - 2 - channels), jnp.float32)
    tail = jnp.zeros((spans, steps, channels, LANES - channels), jnp.float32)
    body = jnp.concatenate(
        [coupling[:, :, 0], gap, rates, gains, coupling[:, :, 1], tail], axis=-1
    )
    body = jnp.pad(body, ((0, 0), (0, 0), (0, rows - channels), (0, 0)))
    lines = jnp.concatenate(
        [
            impulse[..., :1],
            jnp.zeros(impulse.shape[:-1] + (2 * LANES - taps,), jnp.float32),
            impulse[..., :0:-1],
        ],
        axis=-1,
    )
    lines = jnp.pad(lines, ((0, 0), (0, 0), (0, 6), (0, 0)))
    return jnp.concatenate([body, lines], axis=2)


def shards(launched, coupling, impulse, amplifier, nonlinear):
    n_span = lax.axis_size("span")
    n_tm = lax.axis_size("tm")
    frames, _, channels, samples = launched.shape
    _, spans, steps, _, taps = impulse.shape
    per = frames // n_span
    rows = padded_rows(channels)
    edge = steps * (taps - 1) // 2
    rounds = n_span * spans
    pack = packed(coupling[0], impulse[0], amplifier[0], nonlinear[0])
    sizes = (n_span, n_tm, spans, steps, channels, samples, per, edge)
    dma = pltpu.SemaphoreType.DMA
    return pl.pallas_call(
        functools.partial(kernel, sizes),
        out_shape=jax.ShapeDtypeStruct((1,) + launched.shape, jnp.float32),
        in_specs=[pl.BlockSpec(memory_space=pl.ANY)] * 2,
        out_specs=pl.BlockSpec(memory_space=pl.ANY),
        scratch_shapes=[
            pltpu.VMEM((per, 2, channels, samples), jnp.float32),
            pltpu.VMEM((rounds + 1, per, 2 * rows, samples), jnp.float32),
            pltpu.VMEM((rounds, per, 2 * rows, edge), jnp.float32),
            pltpu.VMEM((rounds, per, 2 * rows, edge), jnp.float32),
            pltpu.VMEM((n_span,) + pack.shape, jnp.float32),
            pltpu.VMEM((steps, 2 * rows, 2 * LANES), jnp.bfloat16),
            pltpu.VMEM((steps, 2 * rows, 2 * LANES), jnp.bfloat16),
            pltpu.VMEM((steps, 2 * LANES, 2 * LANES), jnp.bfloat16),
            pltpu.VMEM((steps, 2 * LANES, 2 * LANES), jnp.bfloat16),
            pltpu.VMEM((n_span, per, 2, channels, samples), jnp.float32),
            dma((per,)),
            dma((spans,)),
            dma((spans, n_span)),
            dma((n_span, spans)),
            dma((rounds, per)),
            dma((rounds, per)),
            dma((rounds, per)),
            dma((rounds, per)),
            dma((n_span, per)),
            dma((n_span, per)),
        ],
        compiler_params=pltpu.CompilerParams(
            collective_id=0, has_side_effects=True, vmem_limit_bytes=48 * 1024 * 1024
        ),
        name="link",
    )(launched, pack)


def solution(mesh):
    placed = (
        P(None, None, None, "tm"),
        P("span", None, None, None, None, None),
        P("span", None, None, None, None),
        P("span", None, None),
        P("span", None, None),
    )
    return jax.shard_map(
        shards,
        mesh=mesh,
        in_specs=placed,
        out_specs=P("span", None, None, None, "tm"),
        check_vma=False,
    )
```

```python
import functools

import jax
import jax.numpy as jnp
from jax import lax
from jax.experimental import pallas as pl
from jax.experimental.pallas import tpu as pltpu
from jax.sharding import PartitionSpec as P

MESH = pl.DeviceIdType.MESH
LANES = 128


def padded_rows(channels):
    return (channels + 15) // 16 * 16


def halves(value):
    high = value.astype(jnp.bfloat16)
    low = (value - high.astype(jnp.float32)).astype(jnp.bfloat16)
    return high, low


def product(a, b):
    return jnp.dot(a, b, preferred_element_type=jnp.float32)


def cos_sin(angle):
    turns = jnp.floor(angle * 0.6366197723675814 + 0.5)
    r = angle - turns * 1.5703125
    r = r - turns * 4.837512969970703e-4
    r = r - turns * 7.549789948768648e-8
    z = r * r
    sine = r + r * z * (-1.6666654611e-1 + z * (8.3321608736e-3 - z * 1.9515295891e-4))
    cosine = 1.0 - 0.5 * z + z * z * (
        4.166664568298827e-2 + z * (-1.388731625493765e-3 + z * 2.443315711809948e-5)
    )
    quadrant = turns - 4.0 * jnp.floor(turns * 0.25)
    odd = (quadrant == 1.0) | (quadrant == 3.0)
    cos_sign = jnp.where((quadrant == 1.0) | (quadrant == 2.0), -1.0, 1.0)
    sin_sign = jnp.where(quadrant >= 2.0, -1.0, 1.0)
    return cos_sign * jnp.where(odd, sine, cosine), sin_sign * jnp.where(odd, cosine, sine)


def kernel(
    sizes,
    launched_ref,
    coupling_ref,
    impulse_ref,
    amplifier_ref,
    nonlinear_ref,
    out_ref,
    lstage,
    taps_stage,
    gain_stage,
    rate_stage,
    own,
    low_halo,
    high_halo,
    mixers,
    smalls,
    square,
    mix,
    fir,
    ostage,
    lsem,
    small_load,
    own_mix,
    small_send,
    small_recv,
    mix_send,
    mix_recv,
    share_send,
    share_recv,
    up_send,
    up_recv,
    down_send,
    down_recv,
    out_send,
    out_recv,
):
    n_span, n_tm, spans, steps, channels, samples, per, edge = sizes
    rows = padded_rows(channels)
    gain_row = 2 * spans * steps
    rate_row = gain_row + spans
    rounds = n_span * spans
    me = lax.axis_index("span")
    tm = lax.axis_index("tm")
    above = jnp.minimum(tm + 1, n_tm - 1)
    below = jnp.maximum(tm - 1, 0)
    has_below = tm > 0
    has_above = tm < n_tm - 1

    def load(f):
        return pltpu.make_async_copy(launched_ref.at[me * per + f], lstage.at[f], lsem.at[f])

    core = lax.rem(tm, 2)
    sibling = tm + 1 - 2 * core
    small_loads = [
        pltpu.make_async_copy(impulse_ref.at[0], taps_stage, small_load.at[0]),
        pltpu.make_async_copy(amplifier_ref.at[0], gain_stage, small_load.at[1]),
        pltpu.make_async_copy(nonlinear_ref.at[0], rate_stage, small_load.at[2]),
    ]
    own_mixers = pltpu.make_async_copy(coupling_ref.at[0], mixers.at[me], own_mix)

    def give_small(by):
        return pltpu.make_async_remote_copy(
            src_ref=smalls.at[me],
            dst_ref=smalls.at[me],
            send_sem=small_send.at[by],
            recv_sem=small_recv.at[me],
            device_id={"span": lax.rem(me + by, n_span)},
            device_id_type=MESH,
        )

    def got_small(g):
        return pltpu.make_async_remote_copy(
            src_ref=smalls.at[g],
            dst_ref=smalls.at[g],
            send_sem=small_send.at[1],
            recv_sem=small_recv.at[g],
            device_id={"span": g},
            device_id_type=MESH,
        )

    def give_mix(r, k, by):
        return pltpu.make_async_remote_copy(
            src_ref=coupling_ref.at[0, r, k, core],
            dst_ref=mixers.at[me, r, k, core],
            send_sem=mix_send.at[r, k, by],
            recv_sem=mix_recv.at[me, r, k],
            device_id={"span": lax.rem(me + by, n_span)},
            device_id_type=MESH,
        )

    def got_mix(g, r, k):
        return pltpu.make_async_remote_copy(
            src_ref=coupling_ref.at[0, r, k, core],
            dst_ref=mixers.at[g, r, k, core],
            send_sem=mix_send.at[r, k, 1],
            recv_sem=mix_recv.at[g, r, k],
            device_id={"span": g},
            device_id_type=MESH,
        )

    def share_mix(g, r, k):
        return pltpu.make_async_remote_copy(
            src_ref=mixers.at[g, r, k, core],
            dst_ref=mixers.at[g, r, k, core],
            send_sem=share_send.at[g, r, k],
            recv_sem=share_recv.at[g, r, k],
            device_id={"tm": sibling},
            device_id_type=MESH,
        )

    def shared_mix(g, r, k):
        return pltpu.make_async_remote_copy(
            src_ref=mixers.at[g, r, k, 1 - core],
            dst_ref=mixers.at[g, r, k, 1 - core],
            send_sem=share_send.at[g, r, k],
            recv_sem=share_recv.at[g, r, k],
            device_id={"tm": sibling},
            device_id_type=MESH,
        )

    def give(t):
        r = t % spans

        @pl.when(t // spans == me)
        def _():
            for k in range(steps):
                for by in range(1, n_span):
                    give_mix(r, k, by).start()

    def relay(t):
        g = t // spans
        r = t % spans

        @pl.when(g != me)
        def _():
            for k in range(steps):
                got_mix(g, r, k).wait_recv()
                share_mix(g, r, k).start()

    def go_up(t, f):
        return pltpu.make_async_remote_copy(
            src_ref=own.at[t, f, :, pl.ds(samples - edge, edge)],
            dst_ref=low_halo.at[t, f],
            send_sem=up_send.at[t, f],
            recv_sem=up_recv.at[t, f],
            device_id={"tm": above},
            device_id_type=MESH,
        )

    def go_down(t, f):
        return pltpu.make_async_remote_copy(
            src_ref=own.at[t, f, :, pl.ds(0, edge)],
            dst_ref=high_halo.at[t, f],
            send_sem=down_send.at[t, f],
            recv_sem=down_recv.at[t, f],
            device_id={"tm": below},
            device_id_type=MESH,
        )

    def send_edges(t, f):
        @pl.when(has_above)
        def _():
            go_up(t, f).start()

        @pl.when(has_below)
        def _():
            go_down(t, f).start()

    def keep_out(g, f):
        return pltpu.make_async_copy(
            ostage.at[g, f], out_ref.at[0, me * per + f], out_send.at[g, f]
        )

    def send_out(g, f):
        return pltpu.make_async_remote_copy(
            src_ref=ostage.at[g, f],
            dst_ref=out_ref.at[0, me * per + f],
            send_sem=out_send.at[g, f],
            recv_sem=out_recv.at[me, f],
            device_id={"span": g},
            device_id_type=MESH,
        )

    def got_out(source, f):
        return pltpu.make_async_remote_copy(
            src_ref=ostage.at[0, f],
            dst_ref=out_ref.at[0, source * per + f],
            send_sem=out_send.at[0, f],
            recv_sem=out_recv.at[source, f],
            device_id={"span": source},
            device_id_type=MESH,
        )

    for f in range(per):
        load(f).start()
    for copy in small_loads:
        copy.start()
    own_mixers.start()

    barrier = pltpu.get_barrier_semaphore()
    for by in range(1, n_span):
        pl.semaphore_signal(
            barrier, inc=1, device_id={"span": lax.rem(me + by, n_span)}, device_id_type=MESH
        )

    @pl.when(has_above)
    def _():
        pl.semaphore_signal(barrier, inc=1, device_id={"tm": above}, device_id_type=MESH)

    @pl.when(has_below)
    def _():
        pl.semaphore_signal(barrier, inc=1, device_id={"tm": below}, device_id_type=MESH)

    for f in range(per):
        load(f).wait()
        for part in range(2):
            own[0, f, pl.ds(part * rows + rows - 8, 8), :] = jnp.zeros((8, samples), jnp.float32)
            own[0, f, pl.ds(part * rows, channels), :] = lstage[f, part]

    square[...] = jnp.zeros(square.shape, jnp.float32)
    for copy in small_loads:
        copy.wait()
    smalls[me] = jnp.zeros(smalls.shape[1:], jnp.float32)
    for r in range(spans):
        for k in range(steps):
            first = 2 * (r * steps + k)
            smalls[me, pl.ds(first, 2), : taps_stage.shape[-1]] = taps_stage[r, k]
    smalls[me, pl.ds(gain_row, spans), :channels] = gain_stage[...]
    smalls[me, pl.ds(rate_row, spans), :steps] = rate_stage[...]

    pl.semaphore_wait(
        barrier,
        n_span - 1 + jnp.where(has_above, 1, 0) + jnp.where(has_below, 1, 0),
    )
    give(0)
    for f in range(per):
        send_edges(0, f)
    for by in range(1, n_span):
        give_small(by).start()
    own_mixers.wait()

    def chosen(g, r, first):
        both = smalls[g, pl.ds(first, spans)]
        return jnp.sum(
            jnp.where(lax.broadcasted_iota(jnp.int32, both.shape, 0) == r, both, 0.0),
            axis=0,
            keepdims=True,
        )

    def prepare(t):
        g = t // spans
        r = t % spans

        @pl.when((g != me) & (r == 0))
        def _():
            got_small(g).wait_recv()

        for k in range(steps):

            @pl.when(g != me)
            def _():
                shared_mix(g, r, k).wait_recv()

            real = mixers[g, r, k, 0]
            imag = mixers[g, r, k, 1]
            square[:channels, :channels] = real
            square[:channels, pl.ds(LANES, channels)] = -imag
            square[pl.ds(rows, channels), :channels] = imag
            square[pl.ds(rows, channels), pl.ds(LANES, channels)] = real
            high, low = halves(square[...])
            mix[k, :, pl.ds(0, 2 * LANES)] = high
            mix[k, :, pl.ds(2 * LANES, 2 * LANES)] = high
            mix[k, :, pl.ds(4 * LANES, 2 * LANES)] = low
            pair = smalls[g, pl.ds(0, gain_row)]
            which = lax.broadcasted_iota(jnp.int32, pair.shape, 0)
            for part in range(2):
                line = jnp.sum(
                    jnp.where(which == 2 * (r * steps + k) + part, pair, 0.0),
                    axis=0,
                    keepdims=True,
                )
                line = jnp.broadcast_to(line, (LANES, 2 * LANES))
                band = pltpu.roll(line, 0, 1, stride=1, stride_axis=0)
                column = pl.ds(part * LANES, LANES)
                for half in range(2):
                    high, low = halves(band[:, half * LANES : (half + 1) * LANES].T)
                    fir[k, pl.ds(half * LANES, LANES), column] = high
                    fir[k, pl.ds((2 + half) * LANES, LANES), column] = high
                    fir[k, pl.ds((4 + half) * LANES, LANES), column] = low

    gap = jnp.zeros((LANES - rows, 1), jnp.bfloat16)

    def spread(real, imag):
        fill = jnp.broadcast_to(gap, (LANES - rows, real.shape[1]))
        return jnp.concatenate([real, fill, imag, fill], axis=0)

    def advance(t, f):
        g = t // spans
        r = t % spans
        blocks = (
            [low_halo[t, f, :, pl.ds(i, LANES)] for i in range(0, edge, LANES)]
            + [own[t, f, :, pl.ds(i, LANES)] for i in range(0, samples, LANES)]
            + [high_halo[t, f, :, pl.ds(i, LANES)] for i in range(0, edge, LANES)]
        )
        rates = chosen(g, r, rate_row)
        gain = chosen(g, r, gain_row)[:, :LANES]
        gain = jnp.broadcast_to(gain, (LANES, LANES)).T[:rows, :1]
        margin = edge
        for k in range(steps):
            margin = margin - edge // steps
            split = [halves(block) for block in blocks]
            count = len(blocks) - 1
            high = jnp.concatenate(
                [
                    jnp.concatenate([split[b][0], split[b + 1][0]], axis=1)
                    for b in range(count)
                ],
                axis=0,
            )
            low = jnp.concatenate(
                [
                    jnp.concatenate([split[b][1], split[b + 1][1]], axis=1)
                    for b in range(count)
                ],
                axis=0,
            )
            wide = product(jnp.concatenate([high, low, high], axis=1), fir[k])
            real_parts = []
            imag_parts = []
            for b in range(count):
                top = wide[b * 2 * rows : b * 2 * rows + rows]
                bottom = wide[b * 2 * rows + rows : (b + 1) * 2 * rows]
                real_parts.append(top[:, :LANES] - bottom[:, LANES:])
                imag_parts.append(top[:, LANES:] + bottom[:, :LANES])
            real = jnp.concatenate(real_parts, axis=1)
            imag = jnp.concatenate(imag_parts, axis=1)
            if margin > 0:
                extent = count * LANES
                place = tm * samples - margin + lax.broadcasted_iota(jnp.int32, (1, extent), 1)
                inside = ((place >= 0) & (place < samples * n_tm)).astype(jnp.float32)
                real = real * inside
                imag = imag * inside
            real_high, real_low = halves(real)
            imag_high, imag_low = halves(imag)
            spread_high = spread(real_high, imag_high)
            mixed = product(
                mix[k],
                jnp.concatenate([spread_high, spread(real_low, imag_low), spread_high], axis=0),
            )
            power = jnp.sum(mixed * mixed, axis=0, keepdims=True)
            cosine, sine = cos_sin(power * rates[:, k : k + 1])
            real = mixed[:rows] * cosine - mixed[rows:] * sine
            imag = mixed[:rows] * sine + mixed[rows:] * cosine
            if k == steps - 1:
                real = real * gain
                imag = imag * gain
            both = jnp.concatenate([real, imag], axis=0)
            blocks = [both[:, b * LANES : (b + 1) * LANES] for b in range(count)]
        own[t + 1, f] = both

        @pl.when(t + 1 < rounds)
        def _():
            send_edges(t + 1, f)

        @pl.when(r == spans - 1)
        def _():
            ostage[g, f, 0] = real[:channels]
            ostage[g, f, 1] = imag[:channels]

            @pl.when(g == me)
            def _():
                keep_out(g, f).start()

            @pl.when(g != me)
            def _():
                send_out(g, f).start()

    relay(0)
    prepare(0)
    give(1)

    def one_round(t, carry):
        for f in range(per):

            @pl.when(has_below)
            def _():
                go_up(t, f).wait_recv()

            @pl.when(jnp.logical_not(has_below))
            def _():
                low_halo[t, f] = jnp.zeros(low_halo.shape[2:], jnp.float32)

            @pl.when(has_above)
            def _():
                go_down(t, f).wait_recv()

            @pl.when(jnp.logical_not(has_above))
            def _():
                high_halo[t, f] = jnp.zeros(high_halo.shape[2:], jnp.float32)

            if f == 0:

                @pl.when(t + 2 < rounds)
                def _():
                    give(t + 2)

            advance(t, f)
            if f == 0:

                @pl.when(t + 1 < rounds)
                def _():
                    relay(t + 1)

        @pl.when(t + 1 < rounds)
        def _():
            prepare(t + 1)

        return carry

    lax.fori_loop(0, rounds, one_round, 0)

    def drain(t, carry):
        for f in range(per):

            @pl.when(has_above)
            def _():
                go_up(t, f).wait_send()

            @pl.when(has_below)
            def _():
                go_down(t, f).wait_send()

        return carry

    lax.fori_loop(0, rounds, drain, 0)
    for by in range(1, n_span):
        give_small(by).wait_send()
        for r in range(spans):
            for k in range(steps):
                give_mix(r, k, by).wait_send()

    def drain_shares(t, carry):
        @pl.when(t // spans != me)
        def _():
            for k in range(steps):
                share_mix(t // spans, t % spans, k).wait_send()

        return carry

    lax.fori_loop(0, rounds, drain_shares, 0)

    def finish(g, carry):
        for f in range(per):

            @pl.when(g == me)
            def _():
                keep_out(g, f).wait()

            @pl.when(g != me)
            def _():
                send_out(g, f).wait_send()
                got_out(g, f).wait_recv()

        return carry

    lax.fori_loop(0, n_span, finish, 0)


def shards(launched, coupling, impulse, amplifier, nonlinear):
    n_span = lax.axis_size("span")
    n_tm = lax.axis_size("tm")
    frames, _, channels, samples = launched.shape
    _, spans, steps, _, taps = impulse.shape
    per = frames // n_span
    rows = padded_rows(channels)
    edge = steps * (taps - 1) // 2
    rounds = n_span * spans
    small_rows = (2 * spans * steps + 2 * spans + 7) // 8 * 8
    sizes = (n_span, n_tm, spans, steps, channels, samples, per, edge)
    dma = pltpu.SemaphoreType.DMA
    return pl.pallas_call(
        functools.partial(kernel, sizes),
        out_shape=jax.ShapeDtypeStruct((1,) + launched.shape, jnp.float32),
        in_specs=[pl.BlockSpec(memory_space=pl.ANY)] * 5,
        out_specs=pl.BlockSpec(memory_space=pl.ANY),
        scratch_shapes=[
            pltpu.VMEM((per, 2, channels, samples), jnp.float32),
            pltpu.VMEM(impulse.shape[1:], jnp.float32),
            pltpu.VMEM(amplifier.shape[1:], jnp.float32),
            pltpu.VMEM(nonlinear.shape[1:], jnp.float32),
            pltpu.VMEM((rounds + 1, per, 2 * rows, samples), jnp.float32),
            pltpu.VMEM((rounds, per, 2 * rows, edge), jnp.float32),
            pltpu.VMEM((rounds, per, 2 * rows, edge), jnp.float32),
            pltpu.VMEM((n_span,) + coupling.shape[1:], jnp.float32),
            pltpu.VMEM((n_span, small_rows, 2 * LANES), jnp.float32),
            pltpu.VMEM((2 * rows, 2 * LANES), jnp.float32),
            pltpu.VMEM((steps, 2 * rows, 6 * LANES), jnp.bfloat16),
            pltpu.VMEM((steps, 6 * LANES, 2 * LANES), jnp.bfloat16),
            pltpu.VMEM((n_span, per, 2, channels, samples), jnp.float32),
            dma((per,)),
            dma((3,)),
            dma,
            dma((n_span,)),
            dma((n_span,)),
            dma((spans, steps, n_span)),
            dma((n_span, spans, steps)),
            dma((n_span, spans, steps)),
            dma((n_span, spans, steps)),
            dma((rounds, per)),
            dma((rounds, per)),
            dma((rounds, per)),
            dma((rounds, per)),
            dma((n_span, per)),
            dma((n_span, per)),
        ],
        compiler_params=pltpu.CompilerParams(
            collective_id=0, has_side_effects=True, vmem_limit_bytes=48 * 1024 * 1024
        ),
        name="link",
    )(launched, coupling, impulse, amplifier, nonlinear)


def solution(mesh):
    placed = (
        P(None, None, None, "tm"),
        P("span", None, None, None, None, None),
        P("span", None, None, None, None),
        P("span", None, None),
        P("span", None, None),
    )
    return jax.shard_map(
        shards,
        mesh=mesh,
        in_specs=placed,
        out_specs=P("span", None, None, None, "tm"),
        check_vma=False,
    )
```

```python
import functools

import jax
import jax.numpy as jnp
from jax import lax
from jax.experimental import pallas as pl
from jax.experimental.pallas import tpu as pltpu
from jax.sharding import PartitionSpec as P

MESH = pl.DeviceIdType.MESH
LANES = 128


def padded_rows(channels):
    return (channels + 15) // 16 * 16


def halves(value):
    high = value.astype(jnp.bfloat16)
    low = (value - high.astype(jnp.float32)).astype(jnp.bfloat16)
    return high, low


def product(a, b):
    return jnp.dot(a, b, preferred_element_type=jnp.float32)


def cos_sin(angle):
    turns = jnp.floor(angle * 0.6366197723675814 + 0.5)
    r = angle - turns * 1.5703125
    r = r - turns * 4.837512969970703e-4
    r = r - turns * 7.549789948768648e-8
    z = r * r
    sine = r + r * z * (-1.6666654611e-1 + z * (8.3321608736e-3 - z * 1.9515295891e-4))
    cosine = 1.0 - 0.5 * z + z * z * (
        4.166664568298827e-2 + z * (-1.388731625493765e-3 + z * 2.443315711809948e-5)
    )
    quadrant = turns - 4.0 * jnp.floor(turns * 0.25)
    odd = (quadrant == 1.0) | (quadrant == 3.0)
    cos_sign = jnp.where((quadrant == 1.0) | (quadrant == 2.0), -1.0, 1.0)
    sin_sign = jnp.where(quadrant >= 2.0, -1.0, 1.0)
    return cos_sign * jnp.where(odd, sine, cosine), sin_sign * jnp.where(odd, cosine, sine)


def kernel(
    sizes,
    launched_ref,
    coupling_ref,
    impulse_ref,
    amplifier_ref,
    nonlinear_ref,
    out_ref,
    lstage,
    taps_stage,
    gain_stage,
    rate_stage,
    own,
    low_halo,
    high_halo,
    mixers,
    smalls,
    square,
    mix,
    fir,
    ostage,
    lsem,
    small_load,
    own_mix,
    small_send,
    small_recv,
    mix_send,
    mix_recv,
    share_send,
    share_recv,
    up_send,
    up_recv,
    down_send,
    down_recv,
    out_send,
    out_recv,
):
    n_span, n_tm, spans, steps, channels, samples, per, edge = sizes
    rows = padded_rows(channels)
    gain_row = 2 * spans * steps
    rate_row = gain_row + spans
    rounds = n_span * spans
    me = lax.axis_index("span")
    tm = lax.axis_index("tm")
    above = jnp.minimum(tm + 1, n_tm - 1)
    below = jnp.maximum(tm - 1, 0)
    has_below = tm > 0
    has_above = tm < n_tm - 1

    def load(f):
        return pltpu.make_async_copy(launched_ref.at[f], lstage.at[f], lsem.at[f])

    core = lax.rem(tm, 2)
    sibling = tm + 1 - 2 * core
    small_loads = [
        pltpu.make_async_copy(impulse_ref.at[0], taps_stage, small_load.at[0]),
        pltpu.make_async_copy(amplifier_ref.at[0], gain_stage, small_load.at[1]),
        pltpu.make_async_copy(nonlinear_ref.at[0], rate_stage, small_load.at[2]),
    ]
    own_mixers = pltpu.make_async_copy(coupling_ref.at[0], mixers.at[me], own_mix)

    def give_small(by):
        return pltpu.make_async_remote_copy(
            src_ref=smalls.at[me],
            dst_ref=smalls.at[me],
            send_sem=small_send.at[by],
            recv_sem=small_recv.at[me],
            device_id={"span": lax.rem(me + by, n_span)},
            device_id_type=MESH,
        )

    def got_small(g):
        return pltpu.make_async_remote_copy(
            src_ref=smalls.at[g],
            dst_ref=smalls.at[g],
            send_sem=small_send.at[1],
            recv_sem=small_recv.at[g],
            device_id={"span": g},
            device_id_type=MESH,
        )

    def give_mix(r, k, by):
        return pltpu.make_async_remote_copy(
            src_ref=coupling_ref.at[0, r, k, core],
            dst_ref=mixers.at[me, r, k, core],
            send_sem=mix_send.at[r, k, by],
            recv_sem=mix_recv.at[me, r, k],
            device_id={"span": lax.rem(me + by, n_span)},
            device_id_type=MESH,
        )

    def got_mix(g, r, k):
        return pltpu.make_async_remote_copy(
            src_ref=coupling_ref.at[0, r, k, core],
            dst_ref=mixers.at[g, r, k, core],
            send_sem=mix_send.at[r, k, 1],
            recv_sem=mix_recv.at[g, r, k],
            device_id={"span": g},
            device_id_type=MESH,
        )

    def share_mix(g, r, k):
        return pltpu.make_async_remote_copy(
            src_ref=mixers.at[g, r, k, core],
            dst_ref=mixers.at[g, r, k, core],
            send_sem=share_send.at[g, r, k],
            recv_sem=share_recv.at[g, r, k],
            device_id={"tm": sibling},
            device_id_type=MESH,
        )

    def shared_mix(g, r, k):
        return pltpu.make_async_remote_copy(
            src_ref=mixers.at[g, r, k, 1 - core],
            dst_ref=mixers.at[g, r, k, 1 - core],
            send_sem=share_send.at[g, r, k],
            recv_sem=share_recv.at[g, r, k],
            device_id={"tm": sibling},
            device_id_type=MESH,
        )

    def give(t):
        r = t % spans

        @pl.when(t // spans == me)
        def _():
            for k in range(steps):
                for by in range(1, n_span):
                    give_mix(r, k, by).start()

    def relay(t):
        g = t // spans
        r = t % spans

        @pl.when(g != me)
        def _():
            for k in range(steps):
                got_mix(g, r, k).wait_recv()
                share_mix(g, r, k).start()

    def go_up(t, f):
        return pltpu.make_async_remote_copy(
            src_ref=own.at[t, f, :, pl.ds(samples - edge, edge)],
            dst_ref=low_halo.at[t, f],
            send_sem=up_send.at[t, f],
            recv_sem=up_recv.at[t, f],
            device_id={"tm": above},
            device_id_type=MESH,
        )

    def go_down(t, f):
        return pltpu.make_async_remote_copy(
            src_ref=own.at[t, f, :, pl.ds(0, edge)],
            dst_ref=high_halo.at[t, f],
            send_sem=down_send.at[t, f],
            recv_sem=down_recv.at[t, f],
            device_id={"tm": below},
            device_id_type=MESH,
        )

    def send_edges(t, f):
        @pl.when(has_above)
        def _():
            go_up(t, f).start()

        @pl.when(has_below)
        def _():
            go_down(t, f).start()

    def keep_out(g, f):
        return pltpu.make_async_copy(
            ostage.at[g, f], out_ref.at[0, me * per + f], out_send.at[g, f]
        )

    def send_out(g, f):
        return pltpu.make_async_remote_copy(
            src_ref=ostage.at[g, f],
            dst_ref=out_ref.at[0, me * per + f],
            send_sem=out_send.at[g, f],
            recv_sem=out_recv.at[me, f],
            device_id={"span": g},
            device_id_type=MESH,
        )

    def got_out(source, f):
        return pltpu.make_async_remote_copy(
            src_ref=ostage.at[0, f],
            dst_ref=out_ref.at[0, source * per + f],
            send_sem=out_send.at[0, f],
            recv_sem=out_recv.at[source, f],
            device_id={"span": source},
            device_id_type=MESH,
        )

    for f in range(per):
        load(f).start()
    for copy in small_loads:
        copy.start()
    own_mixers.start()

    barrier = pltpu.get_barrier_semaphore()
    for by in range(1, n_span):
        pl.semaphore_signal(
            barrier, inc=1, device_id={"span": lax.rem(me + by, n_span)}, device_id_type=MESH
        )

    @pl.when(has_above)
    def _():
        pl.semaphore_signal(barrier, inc=1, device_id={"tm": above}, device_id_type=MESH)

    @pl.when(has_below)
    def _():
        pl.semaphore_signal(barrier, inc=1, device_id={"tm": below}, device_id_type=MESH)

    for f in range(per):
        load(f).wait()
        for part in range(2):
            own[0, f, pl.ds(part * rows + rows - 8, 8), :] = jnp.zeros((8, samples), jnp.float32)
            own[0, f, pl.ds(part * rows, channels), :] = lstage[f, part]

    square[...] = jnp.zeros(square.shape, jnp.float32)
    for copy in small_loads:
        copy.wait()
    smalls[me] = jnp.zeros(smalls.shape[1:], jnp.float32)
    for r in range(spans):
        for k in range(steps):
            first = 2 * (r * steps + k)
            smalls[me, pl.ds(first, 2), : taps_stage.shape[-1]] = taps_stage[r, k]
    smalls[me, pl.ds(gain_row, spans), :channels] = gain_stage[...]
    smalls[me, pl.ds(rate_row, spans), :steps] = rate_stage[...]

    pl.semaphore_wait(
        barrier,
        n_span - 1 + jnp.where(has_above, 1, 0) + jnp.where(has_below, 1, 0),
    )
    give(0)
    for f in range(per):
        send_edges(0, f)
    for by in range(1, n_span):
        give_small(by).start()
    own_mixers.wait()

    def chosen(g, r, first):
        both = smalls[g, pl.ds(first, spans)]
        return jnp.sum(
            jnp.where(lax.broadcasted_iota(jnp.int32, both.shape, 0) == r, both, 0.0),
            axis=0,
            keepdims=True,
        )

    def prepare(t):
        g = t // spans
        r = t % spans

        @pl.when((g != me) & (r == 0))
        def _():
            got_small(g).wait_recv()

        for k in range(steps):

            @pl.when(g != me)
            def _():
                shared_mix(g, r, k).wait_recv()

            real = mixers[g, r, k, 0]
            imag = mixers[g, r, k, 1]
            square[:channels, :channels] = real
            square[:channels, pl.ds(LANES, channels)] = -imag
            square[pl.ds(rows, channels), :channels] = imag
            square[pl.ds(rows, channels), pl.ds(LANES, channels)] = real
            high, low = halves(square[...])
            mix[k, :, pl.ds(0, 2 * LANES)] = high
            mix[k, :, pl.ds(2 * LANES, 2 * LANES)] = high
            mix[k, :, pl.ds(4 * LANES, 2 * LANES)] = low
            pair = smalls[g, pl.ds(0, gain_row)]
            which = lax.broadcasted_iota(jnp.int32, pair.shape, 0)
            for part in range(2):
                line = jnp.sum(
                    jnp.where(which == 2 * (r * steps + k) + part, pair, 0.0),
                    axis=0,
                    keepdims=True,
                )
                line = jnp.broadcast_to(line, (LANES, 2 * LANES))
                band = pltpu.roll(line, 0, 1, stride=1, stride_axis=0)
                column = pl.ds(part * LANES, LANES)
                for half in range(2):
                    high, low = halves(band[:, half * LANES : (half + 1) * LANES].T)
                    fir[k, pl.ds(half * LANES, LANES), column] = high
                    fir[k, pl.ds((2 + half) * LANES, LANES), column] = high
                    fir[k, pl.ds((4 + half) * LANES, LANES), column] = low

    gap = jnp.zeros((LANES - rows, 1), jnp.bfloat16)

    def spread(real, imag):
        fill = jnp.broadcast_to(gap, (LANES - rows, real.shape[1]))
        return jnp.concatenate([real, fill, imag, fill], axis=0)

    def advance(t):
        g = t // spans
        r = t % spans
        runs = [
            [low_halo[t, f, :, pl.ds(i, LANES)] for i in range(0, edge, LANES)]
            + [own[t, f, :, pl.ds(i, LANES)] for i in range(0, samples, LANES)]
            + [high_halo[t, f, :, pl.ds(i, LANES)] for i in range(0, edge, LANES)]
            for f in range(per)
        ]
        rates = chosen(g, r, rate_row)
        gain = chosen(g, r, gain_row)[:, :LANES]
        gain = jnp.broadcast_to(gain, (LANES, LANES)).T[:rows]
        margin = edge
        for k in range(steps):
            margin = margin - edge // steps
            count = len(runs[0]) - 1
            high = []
            low = []
            for run in runs:
                split = [halves(block) for block in run]
                for b in range(count):
                    high.append(jnp.concatenate([split[b][0], split[b + 1][0]], axis=1))
                    low.append(jnp.concatenate([split[b][1], split[b + 1][1]], axis=1))
            high = jnp.concatenate(high, axis=0)
            low = jnp.concatenate(low, axis=0)
            wide = product(jnp.concatenate([high, low, high], axis=1), fir[k])
            spread_high = []
            spread_low = []
            for f in range(per):
                for b in range(count):
                    first = (f * count + b) * 2 * rows
                    top = wide[first : first + rows]
                    bottom = wide[first + rows : first + 2 * rows]
                    real = top[:, :LANES] - bottom[:, LANES:]
                    imag = top[:, LANES:] + bottom[:, :LANES]
                    if b * LANES < margin or (b + 1) * LANES > margin + samples:
                        place = (
                            tm * samples
                            - margin
                            + b * LANES
                            + lax.broadcasted_iota(jnp.int32, (1, LANES), 1)
                        )
                        inside = ((place >= 0) & (place < samples * n_tm)).astype(jnp.float32)
                        real = real * inside
                        imag = imag * inside
                    real_high, real_low = halves(real)
                    imag_high, imag_low = halves(imag)
                    spread_high.append(spread(real_high, imag_high))
                    spread_low.append(spread(real_low, imag_low))
            spread_high = jnp.concatenate(spread_high, axis=1)
            spread_low = jnp.concatenate(spread_low, axis=1)
            mixed = product(
                mix[k], jnp.concatenate([spread_high, spread_low, spread_high], axis=0)
            )
            power = jnp.sum(mixed * mixed, axis=0, keepdims=True)
            cosine, sine = cos_sin(power * rates[:, k : k + 1])
            runs = []
            for f in range(per):
                run = []
                for b in range(count):
                    lanes = slice((f * count + b) * LANES, (f * count + b + 1) * LANES)
                    real = mixed[:rows, lanes]
                    imag = mixed[rows:, lanes]
                    real, imag = (
                        real * cosine[:, lanes] - imag * sine[:, lanes],
                        real * sine[:, lanes] + imag * cosine[:, lanes],
                    )
                    if k == steps - 1:
                        real = real * gain
                        imag = imag * gain
                    run.append(jnp.concatenate([real, imag], axis=0))
                runs.append(run)
        for f in range(per):
            for b in range(count):
                own[t + 1, f, :, pl.ds(b * LANES, LANES)] = runs[f][b]

        @pl.when(t + 1 < rounds)
        def _():
            for f in range(per):
                send_edges(t + 1, f)

        @pl.when(r == spans - 1)
        def _():
            for f in range(per):
                for b in range(count):
                    lanes = pl.ds(b * LANES, LANES)
                    ostage[g, f, 0, :, lanes] = own[t + 1, f, pl.ds(0, channels), lanes]
                    ostage[g, f, 1, :, lanes] = own[t + 1, f, pl.ds(rows, channels), lanes]

                @pl.when(g == me)
                def _():
                    keep_out(g, f).start()

                @pl.when(g != me)
                def _():
                    send_out(g, f).start()

    relay(0)
    prepare(0)
    for t in range(1, rounds):
        give(t)

    def one_round(t, carry):
        for f in range(per):

            @pl.when(has_below)
            def _():
                go_up(t, f).wait_recv()

            @pl.when(jnp.logical_not(has_below))
            def _():
                low_halo[t, f] = jnp.zeros(low_halo.shape[2:], jnp.float32)

            @pl.when(has_above)
            def _():
                go_down(t, f).wait_recv()

            @pl.when(jnp.logical_not(has_above))
            def _():
                high_halo[t, f] = jnp.zeros(high_halo.shape[2:], jnp.float32)

        @pl.when((t > 0) & (t + 1 < rounds))
        def _():
            relay(t + 1)

        advance(t)

        @pl.when(t == 0)
        def _():
            relay(1)

        @pl.when(t + 1 < rounds)
        def _():
            prepare(t + 1)

        return carry

    lax.fori_loop(0, rounds, one_round, 0)

    def drain(t, carry):
        for f in range(per):

            @pl.when(has_above)
            def _():
                go_up(t, f).wait_send()

            @pl.when(has_below)
            def _():
                go_down(t, f).wait_send()

        return carry

    lax.fori_loop(0, rounds, drain, 0)
    for by in range(1, n_span):
        give_small(by).wait_send()
        for r in range(spans):
            for k in range(steps):
                give_mix(r, k, by).wait_send()

    def drain_shares(t, carry):
        @pl.when(t // spans != me)
        def _():
            for k in range(steps):
                share_mix(t // spans, t % spans, k).wait_send()

        return carry

    lax.fori_loop(0, rounds, drain_shares, 0)

    def finish(g, carry):
        for f in range(per):

            @pl.when(g == me)
            def _():
                keep_out(g, f).wait()

            @pl.when(g != me)
            def _():
                send_out(g, f).wait_send()
                got_out(g, f).wait_recv()

        return carry

    lax.fori_loop(0, n_span, finish, 0)


def shards(launched, coupling, impulse, amplifier, nonlinear):
    n_span = lax.axis_size("span")
    n_tm = lax.axis_size("tm")
    frames, _, channels, samples = launched.shape
    _, spans, steps, _, taps = impulse.shape
    per = frames // n_span
    rows = padded_rows(channels)
    edge = steps * (taps - 1) // 2
    rounds = n_span * spans
    small_rows = (2 * spans * steps + 2 * spans + 7) // 8 * 8
    sizes = (n_span, n_tm, spans, steps, channels, samples, per, edge)
    mine = lax.dynamic_slice_in_dim(launched, lax.axis_index("span") * per, per, 0)
    dma = pltpu.SemaphoreType.DMA
    return pl.pallas_call(
        functools.partial(kernel, sizes),
        out_shape=jax.ShapeDtypeStruct((1,) + launched.shape, jnp.float32),
        in_specs=[pl.BlockSpec(memory_space=pl.ANY)] * 5,
        out_specs=pl.BlockSpec(memory_space=pl.ANY),
        scratch_shapes=[
            pltpu.VMEM((per, 2, channels, samples), jnp.float32),
            pltpu.VMEM(impulse.shape[1:], jnp.float32),
            pltpu.VMEM(amplifier.shape[1:], jnp.float32),
            pltpu.VMEM(nonlinear.shape[1:], jnp.float32),
            pltpu.VMEM((rounds + 1, per, 2 * rows, samples), jnp.float32),
            pltpu.VMEM((rounds, per, 2 * rows, edge), jnp.float32),
            pltpu.VMEM((rounds, per, 2 * rows, edge), jnp.float32),
            pltpu.VMEM((n_span,) + coupling.shape[1:], jnp.float32),
            pltpu.VMEM((n_span, small_rows, 2 * LANES), jnp.float32),
            pltpu.VMEM((2 * rows, 2 * LANES), jnp.float32),
            pltpu.VMEM((steps, 2 * rows, 6 * LANES), jnp.bfloat16),
            pltpu.VMEM((steps, 6 * LANES, 2 * LANES), jnp.bfloat16),
            pltpu.VMEM((n_span, per, 2, channels, samples), jnp.float32),
            dma((per,)),
            dma((3,)),
            dma,
            dma((n_span,)),
            dma((n_span,)),
            dma((spans, steps, n_span)),
            dma((n_span, spans, steps)),
            dma((n_span, spans, steps)),
            dma((n_span, spans, steps)),
            dma((rounds, per)),
            dma((rounds, per)),
            dma((rounds, per)),
            dma((rounds, per)),
            dma((n_span, per)),
            dma((n_span, per)),
        ],
        compiler_params=pltpu.CompilerParams(
            collective_id=0, has_side_effects=True, vmem_limit_bytes=48 * 1024 * 1024
        ),
        name="link",
    )(mine, coupling, impulse, amplifier, nonlinear)


def solution(mesh):
    placed = (
        P(None, None, None, "tm"),
        P("span", None, None, None, None, None),
        P("span", None, None, None, None),
        P("span", None, None),
        P("span", None, None),
    )
    return jax.shard_map(
        shards,
        mesh=mesh,
        in_specs=placed,
        out_specs=P("span", None, None, None, "tm"),
        check_vma=False,
    )
```

```python
import functools

import jax
import jax.numpy as jnp
from jax import lax
from jax.experimental import pallas as pl
from jax.experimental.pallas import tpu as pltpu
from jax.sharding import PartitionSpec as P

MESH = pl.DeviceIdType.MESH
LANES = 128


def padded_rows(channels):
    return (channels + 15) // 16 * 16


def halves(value):
    high = value.astype(jnp.bfloat16)
    low = (value - high.astype(jnp.float32)).astype(jnp.bfloat16)
    return high, low


def product(a_high, a_low, b_high, b_low):
    def dot(a, b):
        return jnp.dot(a, b, preferred_element_type=jnp.float32)

    return dot(a_high, b_high) + dot(a_low, b_high) + dot(a_high, b_low)


def cos_sin(angle):
    turns = jnp.floor(angle * 0.6366197723675814 + 0.5)
    r = angle - turns * 1.5703125
    r = r - turns * 4.837512969970703e-4
    r = r - turns * 7.549789948768648e-8
    z = r * r
    sine = r + r * z * (-1.6666654611e-1 + z * (8.3321608736e-3 - z * 1.9515295891e-4))
    cosine = 1.0 - 0.5 * z + z * z * (
        4.166664568298827e-2 + z * (-1.388731625493765e-3 + z * 2.443315711809948e-5)
    )
    quadrant = turns - 4.0 * jnp.floor(turns * 0.25)
    odd = (quadrant == 1.0) | (quadrant == 3.0)
    cos_sign = jnp.where((quadrant == 1.0) | (quadrant == 2.0), -1.0, 1.0)
    sin_sign = jnp.where(quadrant >= 2.0, -1.0, 1.0)
    return cos_sign * jnp.where(odd, sine, cosine), sin_sign * jnp.where(odd, cosine, sine)


def kernel(
    sizes,
    launched_ref,
    coupling_ref,
    impulse_ref,
    amplifier_ref,
    nonlinear_ref,
    out_ref,
    lstage,
    taps_stage,
    gain_stage,
    rate_stage,
    own,
    low_halo,
    high_halo,
    mixers,
    smalls,
    square,
    mix,
    fir,
    ostage,
    lsem,
    small_load,
    own_mix,
    small_send,
    small_recv,
    mix_send,
    mix_recv,
    share_send,
    share_recv,
    up_send,
    up_recv,
    down_send,
    down_recv,
    out_send,
    out_recv,
):
    n_span, n_tm, spans, steps, channels, samples, per, edge = sizes
    rows = padded_rows(channels)
    gain_row = 2 * spans * steps
    rate_row = gain_row + spans
    rounds = n_span * spans
    me = lax.axis_index("span")
    tm = lax.axis_index("tm")
    above = jnp.minimum(tm + 1, n_tm - 1)
    below = jnp.maximum(tm - 1, 0)
    has_below = tm > 0
    has_above = tm < n_tm - 1

    def load(f):
        return pltpu.make_async_copy(launched_ref.at[f], lstage.at[f], lsem.at[f])

    core = lax.rem(tm, 2)
    sibling = tm + 1 - 2 * core
    small_loads = [
        pltpu.make_async_copy(impulse_ref.at[0], taps_stage, small_load.at[0]),
        pltpu.make_async_copy(amplifier_ref.at[0], gain_stage, small_load.at[1]),
        pltpu.make_async_copy(nonlinear_ref.at[0], rate_stage, small_load.at[2]),
    ]
    own_mixers = pltpu.make_async_copy(coupling_ref.at[0], mixers.at[me], own_mix)

    def give_small(by):
        return pltpu.make_async_remote_copy(
            src_ref=smalls.at[me],
            dst_ref=smalls.at[me],
            send_sem=small_send.at[by],
            recv_sem=small_recv.at[me],
            device_id={"span": lax.rem(me + by, n_span)},
            device_id_type=MESH,
        )

    def got_small(g):
        return pltpu.make_async_remote_copy(
            src_ref=smalls.at[g],
            dst_ref=smalls.at[g],
            send_sem=small_send.at[1],
            recv_sem=small_recv.at[g],
            device_id={"span": g},
            device_id_type=MESH,
        )

    def give_mix(r, k, by):
        return pltpu.make_async_remote_copy(
            src_ref=coupling_ref.at[0, r, k, core],
            dst_ref=mixers.at[me, r, k, core],
            send_sem=mix_send.at[r, k, by],
            recv_sem=mix_recv.at[me, r, k],
            device_id={"span": lax.rem(me + by, n_span)},
            device_id_type=MESH,
        )

    def got_mix(g, r, k):
        return pltpu.make_async_remote_copy(
            src_ref=coupling_ref.at[0, r, k, core],
            dst_ref=mixers.at[g, r, k, core],
            send_sem=mix_send.at[r, k, 1],
            recv_sem=mix_recv.at[g, r, k],
            device_id={"span": g},
            device_id_type=MESH,
        )

    def share_mix(g, r, k):
        return pltpu.make_async_remote_copy(
            src_ref=mixers.at[g, r, k, core],
            dst_ref=mixers.at[g, r, k, core],
            send_sem=share_send.at[g, r, k],
            recv_sem=share_recv.at[g, r, k],
            device_id={"tm": sibling},
            device_id_type=MESH,
        )

    def shared_mix(g, r, k):
        return pltpu.make_async_remote_copy(
            src_ref=mixers.at[g, r, k, 1 - core],
            dst_ref=mixers.at[g, r, k, 1 - core],
            send_sem=share_send.at[g, r, k],
            recv_sem=share_recv.at[g, r, k],
            device_id={"tm": sibling},
            device_id_type=MESH,
        )

    def give(t):
        r = t % spans

        @pl.when(t // spans == me)
        def _():
            for k in range(steps):
                for by in range(1, n_span):
                    give_mix(r, k, by).start()

    def relay(t):
        g = t // spans
        r = t % spans

        @pl.when(g != me)
        def _():
            for k in range(steps):
                got_mix(g, r, k).wait_recv()
                share_mix(g, r, k).start()

    def go_up(t, f):
        return pltpu.make_async_remote_copy(
            src_ref=own.at[t, f, :, pl.ds(samples - edge, edge)],
            dst_ref=low_halo.at[t, f],
            send_sem=up_send.at[t, f],
            recv_sem=up_recv.at[t, f],
            device_id={"tm": above},
            device_id_type=MESH,
        )

    def go_down(t, f):
        return pltpu.make_async_remote_copy(
            src_ref=own.at[t, f, :, pl.ds(0, edge)],
            dst_ref=high_halo.at[t, f],
            send_sem=down_send.at[t, f],
            recv_sem=down_recv.at[t, f],
            device_id={"tm": below},
            device_id_type=MESH,
        )

    def send_edges(t, f):
        @pl.when(has_above)
        def _():
            go_up(t, f).start()

        @pl.when(has_below)
        def _():
            go_down(t, f).start()

    def keep_out(g, f):
        return pltpu.make_async_copy(
            ostage.at[g, f], out_ref.at[0, me * per + f], out_send.at[g, f]
        )

    def send_out(g, f):
        return pltpu.make_async_remote_copy(
            src_ref=ostage.at[g, f],
            dst_ref=out_ref.at[0, me * per + f],
            send_sem=out_send.at[g, f],
            recv_sem=out_recv.at[me, f],
            device_id={"span": g},
            device_id_type=MESH,
        )

    def got_out(source, f):
        return pltpu.make_async_remote_copy(
            src_ref=ostage.at[0, f],
            dst_ref=out_ref.at[0, source * per + f],
            send_sem=out_send.at[0, f],
            recv_sem=out_recv.at[source, f],
            device_id={"span": source},
            device_id_type=MESH,
        )

    for f in range(per):
        load(f).start()
    for copy in small_loads:
        copy.start()
    own_mixers.start()

    barrier = pltpu.get_barrier_semaphore()
    for by in range(1, n_span):
        pl.semaphore_signal(
            barrier, inc=1, device_id={"span": lax.rem(me + by, n_span)}, device_id_type=MESH
        )

    @pl.when(has_above)
    def _():
        pl.semaphore_signal(barrier, inc=1, device_id={"tm": above}, device_id_type=MESH)

    @pl.when(has_below)
    def _():
        pl.semaphore_signal(barrier, inc=1, device_id={"tm": below}, device_id_type=MESH)

    for f in range(per):
        load(f).wait()
        for part in range(2):
            own[0, f, pl.ds(part * rows + rows - 8, 8), :] = jnp.zeros((8, samples), jnp.float32)
            own[0, f, pl.ds(part * rows, channels), :] = lstage[f, part]

    square[...] = jnp.zeros(square.shape, jnp.float32)
    for copy in small_loads:
        copy.wait()
    smalls[me] = jnp.zeros(smalls.shape[1:], jnp.float32)
    for r in range(spans):
        for k in range(steps):
            first = 2 * (r * steps + k)
            smalls[me, pl.ds(first, 2), : taps_stage.shape[-1]] = taps_stage[r, k]
    row = lax.broadcasted_iota(jnp.int32, (2 * LANES, 2 * LANES), 0)
    column = lax.broadcasted_iota(jnp.int32, (2 * LANES, 2 * LANES), 1)
    turned = jnp.where((row + column == 0) | (row + column == 2 * LANES), 1.0, 0.0)
    smalls[me, :gain_row] = jnp.dot(
        smalls[me, :gain_row],
        turned,
        precision=lax.Precision.HIGHEST,
        preferred_element_type=jnp.float32,
    )
    smalls[me, pl.ds(gain_row, spans), :channels] = gain_stage[...]
    smalls[me, pl.ds(rate_row, spans), :steps] = rate_stage[...]

    pl.semaphore_wait(
        barrier,
        n_span - 1 + jnp.where(has_above, 1, 0) + jnp.where(has_below, 1, 0),
    )
    give(0)
    for f in range(per):
        send_edges(0, f)
    for by in range(1, n_span):
        give_small(by).start()
    own_mixers.wait()

    def chosen(g, r, first):
        both = smalls[g, pl.ds(first, spans)]
        return jnp.sum(
            jnp.where(lax.broadcasted_iota(jnp.int32, both.shape, 0) == r, both, 0.0),
            axis=0,
            keepdims=True,
        )

    def prepare(t):
        g = t // spans
        r = t % spans

        @pl.when((g != me) & (r == 0))
        def _():
            got_small(g).wait_recv()

        for k in range(steps):

            @pl.when(g != me)
            def _():
                shared_mix(g, r, k).wait_recv()

            real = mixers[g, r, k, 0]
            imag = mixers[g, r, k, 1]
            square[:channels, :channels] = real
            square[:channels, pl.ds(LANES, channels)] = -imag
            square[pl.ds(rows, channels), :channels] = imag
            square[pl.ds(rows, channels), pl.ds(LANES, channels)] = real
            high, low = halves(square[...])
            mix[0, k] = high
            mix[1, k] = low
            pair = smalls[g, pl.ds(0, gain_row)]
            which = lax.broadcasted_iota(jnp.int32, pair.shape, 0)
            for part in range(2):
                line = jnp.sum(
                    jnp.where(which == 2 * (r * steps + k) + part, pair, 0.0),
                    axis=0,
                    keepdims=True,
                )
                line = jnp.broadcast_to(line, (LANES, 2 * LANES))
                band = pltpu.roll(line, 0, 1, stride=1, stride_axis=0)
                column = pl.ds(part * LANES, LANES)
                high, low = halves(band)
                for half in range(2):
                    place = pl.ds(half * LANES, LANES)
                    fir[0, k, place, column] = high[:, half * LANES : (half + 1) * LANES]
                    fir[1, k, place, column] = low[:, half * LANES : (half + 1) * LANES]

    gap = jnp.zeros((LANES - rows, 1), jnp.bfloat16)

    def spread(real, imag):
        fill = jnp.broadcast_to(gap, (LANES - rows, real.shape[1]))
        return jnp.concatenate([real, fill, imag, fill], axis=0)

    def advance(t, f):
        g = t // spans
        r = t % spans
        blocks = (
            [low_halo[t, f, :, pl.ds(i, LANES)] for i in range(0, edge, LANES)]
            + [own[t, f, :, pl.ds(i, LANES)] for i in range(0, samples, LANES)]
            + [high_halo[t, f, :, pl.ds(i, LANES)] for i in range(0, edge, LANES)]
        )
        rates = chosen(g, r, rate_row)
        gain = chosen(g, r, gain_row)[:, :LANES]
        gain = jnp.broadcast_to(gain, (LANES, LANES)).T[:rows]
        gain = jnp.concatenate([gain] * (samples // LANES), axis=1)
        margin = edge
        for k in range(steps):
            margin = margin - edge // steps
            split = [halves(block) for block in blocks]
            count = len(blocks) - 1
            high = jnp.concatenate(
                [
                    jnp.concatenate([split[b][0], split[b + 1][0]], axis=1)
                    for b in range(count)
                ],
                axis=0,
            )
            low = jnp.concatenate(
                [
                    jnp.concatenate([split[b][1], split[b + 1][1]], axis=1)
                    for b in range(count)
                ],
                axis=0,
            )
            wide = product(high, low, fir[0, k], fir[1, k])
            real_parts = []
            imag_parts = []
            for b in range(count):
                top = wide[b * 2 * rows : b * 2 * rows + rows]
                bottom = wide[b * 2 * rows + rows : (b + 1) * 2 * rows]
                real_parts.append(top[:, :LANES] - bottom[:, LANES:])
                imag_parts.append(top[:, LANES:] + bottom[:, :LANES])
            real = jnp.concatenate(real_parts, axis=1)
            imag = jnp.concatenate(imag_parts, axis=1)
            if margin > 0:
                extent = count * LANES
                place = tm * samples - margin + lax.broadcasted_iota(jnp.int32, (1, extent), 1)
                inside = ((place >= 0) & (place < samples * n_tm)).astype(jnp.float32)
                real = real * inside
                imag = imag * inside
            real_high, real_low = halves(real)
            imag_high, imag_low = halves(imag)
            mixed = product(
                mix[0, k],
                mix[1, k],
                spread(real_high, imag_high),
                spread(real_low, imag_low),
            )
            power = jnp.sum(mixed * mixed, axis=0, keepdims=True)
            cosine, sine = cos_sin(power * rates[:, k : k + 1])
            real = mixed[:rows] * cosine - mixed[rows:] * sine
            imag = mixed[:rows] * sine + mixed[rows:] * cosine
            if k == steps - 1:
                real = real * gain
                imag = imag * gain
            both = jnp.concatenate([real, imag], axis=0)
            blocks = [both[:, b * LANES : (b + 1) * LANES] for b in range(count)]
        own[t + 1, f] = both

        @pl.when(t + 1 < rounds)
        def _():
            send_edges(t + 1, f)

        @pl.when(r == spans - 1)
        def _():
            ostage[g, f, 0] = real[:channels]
            ostage[g, f, 1] = imag[:channels]

            @pl.when(g == me)
            def _():
                keep_out(g, f).start()

            @pl.when(g != me)
            def _():
                send_out(g, f).start()

    relay(0)
    prepare(0)
    for t in range(1, rounds):
        give(t)

    def one_round(t, carry):
        for f in range(per):

            @pl.when(has_below)
            def _():
                go_up(t, f).wait_recv()

            @pl.when(jnp.logical_not(has_below))
            def _():
                low_halo[t, f] = jnp.zeros(low_halo.shape[2:], jnp.float32)

            @pl.when(has_above)
            def _():
                go_down(t, f).wait_recv()

            @pl.when(jnp.logical_not(has_above))
            def _():
                high_halo[t, f] = jnp.zeros(high_halo.shape[2:], jnp.float32)

            advance(t, f)
            if f == 0:

                @pl.when(t + 1 < rounds)
                def _():
                    relay(t + 1)

        @pl.when(t + 1 < rounds)
        def _():
            prepare(t + 1)

        return carry

    lax.fori_loop(0, rounds, one_round, 0)

    def drain(t, carry):
        for f in range(per):

            @pl.when(has_above)
            def _():
                go_up(t, f).wait_send()

            @pl.when(has_below)
            def _():
                go_down(t, f).wait_send()

        return carry

    lax.fori_loop(0, rounds, drain, 0)
    for by in range(1, n_span):
        give_small(by).wait_send()
        for r in range(spans):
            for k in range(steps):
                give_mix(r, k, by).wait_send()

    def drain_shares(t, carry):
        @pl.when(t // spans != me)
        def _():
            for k in range(steps):
                share_mix(t // spans, t % spans, k).wait_send()

        return carry

    lax.fori_loop(0, rounds, drain_shares, 0)

    def finish(g, carry):
        for f in range(per):

            @pl.when(g == me)
            def _():
                keep_out(g, f).wait()

            @pl.when(g != me)
            def _():
                send_out(g, f).wait_send()
                got_out(g, f).wait_recv()

        return carry

    lax.fori_loop(0, n_span, finish, 0)


def shards(launched, coupling, impulse, amplifier, nonlinear):
    n_span = lax.axis_size("span")
    n_tm = lax.axis_size("tm")
    frames, _, channels, samples = launched.shape
    _, spans, steps, _, taps = impulse.shape
    per = frames // n_span
    rows = padded_rows(channels)
    edge = steps * (taps - 1) // 2
    rounds = n_span * spans
    small_rows = (2 * spans * steps + 2 * spans + 7) // 8 * 8
    sizes = (n_span, n_tm, spans, steps, channels, samples, per, edge)
    mine = lax.dynamic_slice_in_dim(launched, lax.axis_index("span") * per, per, 0)
    dma = pltpu.SemaphoreType.DMA
    return pl.pallas_call(
        functools.partial(kernel, sizes),
        out_shape=jax.ShapeDtypeStruct((1,) + launched.shape, jnp.float32),
        in_specs=[pl.BlockSpec(memory_space=pl.ANY)] * 5,
        out_specs=pl.BlockSpec(memory_space=pl.ANY),
        scratch_shapes=[
            pltpu.VMEM((per, 2, channels, samples), jnp.float32),
            pltpu.VMEM(impulse.shape[1:], jnp.float32),
            pltpu.VMEM(amplifier.shape[1:], jnp.float32),
            pltpu.VMEM(nonlinear.shape[1:], jnp.float32),
            pltpu.VMEM((rounds + 1, per, 2 * rows, samples), jnp.float32),
            pltpu.VMEM((rounds, per, 2 * rows, edge), jnp.float32),
            pltpu.VMEM((rounds, per, 2 * rows, edge), jnp.float32),
            pltpu.VMEM((n_span,) + coupling.shape[1:], jnp.float32),
            pltpu.VMEM((n_span, small_rows, 2 * LANES), jnp.float32),
            pltpu.VMEM((2 * rows, 2 * LANES), jnp.float32),
            pltpu.VMEM((2, steps, 2 * rows, 2 * LANES), jnp.bfloat16),
            pltpu.VMEM((2, steps, 2 * LANES, 2 * LANES), jnp.bfloat16),
            pltpu.VMEM((n_span, per, 2, channels, samples), jnp.float32),
            dma((per,)),
            dma((3,)),
            dma,
            dma((n_span,)),
            dma((n_span,)),
            dma((spans, steps, n_span)),
            dma((n_span, spans, steps)),
            dma((n_span, spans, steps)),
            dma((n_span, spans, steps)),
            dma((rounds, per)),
            dma((rounds, per)),
            dma((rounds, per)),
            dma((rounds, per)),
            dma((n_span, per)),
            dma((n_span, per)),
        ],
        compiler_params=pltpu.CompilerParams(
            collective_id=0, has_side_effects=True, vmem_limit_bytes=48 * 1024 * 1024
        ),
        name="link",
    )(mine, coupling, impulse, amplifier, nonlinear)


def solution(mesh):
    placed = (
        P(None, None, None, "tm"),
        P("span", None, None, None, None, None),
        P("span", None, None, None, None),
        P("span", None, None),
        P("span", None, None),
    )
    return jax.shard_map(
        shards,
        mesh=mesh,
        in_specs=placed,
        out_specs=P("span", None, None, None, "tm"),
        check_vma=False,
    )
```

```python
import functools

import jax
import jax.numpy as jnp
from jax import lax
from jax.experimental import pallas as pl
from jax.experimental.pallas import tpu as pltpu
from jax.sharding import PartitionSpec as P

MESH = pl.DeviceIdType.MESH
LANES = 128


def padded_rows(channels):
    return (channels + 15) // 16 * 16


def halves(value):
    high = value.astype(jnp.bfloat16)
    low = (value - high.astype(jnp.float32)).astype(jnp.bfloat16)
    return high, low


def product(a_high, a_low, b_high, b_low):
    def dot(a, b):
        return jnp.dot(a, b, preferred_element_type=jnp.float32)

    return dot(a_high, b_high) + dot(a_low, b_high) + dot(a_high, b_low)


def cos_sin(angle):
    turns = jnp.floor(angle * 0.6366197723675814 + 0.5)
    r = angle - turns * 1.5703125
    r = r - turns * 4.837512969970703e-4
    r = r - turns * 7.549789948768648e-8
    z = r * r
    sine = r + r * z * (-1.6666654611e-1 + z * (8.3321608736e-3 - z * 1.9515295891e-4))
    cosine = 1.0 - 0.5 * z + z * z * (
        4.166664568298827e-2 + z * (-1.388731625493765e-3 + z * 2.443315711809948e-5)
    )
    quadrant = turns - 4.0 * jnp.floor(turns * 0.25)
    odd = (quadrant == 1.0) | (quadrant == 3.0)
    cos_sign = jnp.where((quadrant == 1.0) | (quadrant == 2.0), -1.0, 1.0)
    sin_sign = jnp.where(quadrant >= 2.0, -1.0, 1.0)
    return cos_sign * jnp.where(odd, sine, cosine), sin_sign * jnp.where(odd, cosine, sine)


def kernel(
    sizes,
    launched_ref,
    coupling_ref,
    impulse_ref,
    amplifier_ref,
    nonlinear_ref,
    out_ref,
    lstage,
    taps_stage,
    gain_stage,
    rate_stage,
    own,
    low_halo,
    high_halo,
    mixers,
    smalls,
    square,
    mix,
    fir,
    ostage,
    lsem,
    small_load,
    own_mix,
    small_send,
    small_recv,
    mix_send,
    mix_recv,
    share_send,
    share_recv,
    up_send,
    up_recv,
    down_send,
    down_recv,
    out_send,
    out_recv,
):
    n_span, n_tm, spans, steps, channels, samples, per, edge = sizes
    rows = padded_rows(channels)
    gain_row = 2 * spans * steps
    rate_row = gain_row + spans
    rounds = n_span * spans
    me = lax.axis_index("span")
    tm = lax.axis_index("tm")
    above = jnp.minimum(tm + 1, n_tm - 1)
    below = jnp.maximum(tm - 1, 0)
    has_below = tm > 0
    has_above = tm < n_tm - 1

    def load(f):
        return pltpu.make_async_copy(launched_ref.at[f], lstage.at[f], lsem.at[f])

    core = lax.rem(tm, 2)
    sibling = tm + 1 - 2 * core
    small_loads = [
        pltpu.make_async_copy(impulse_ref.at[0], taps_stage, small_load.at[0]),
        pltpu.make_async_copy(amplifier_ref.at[0], gain_stage, small_load.at[1]),
        pltpu.make_async_copy(nonlinear_ref.at[0], rate_stage, small_load.at[2]),
    ]
    own_mixers = pltpu.make_async_copy(coupling_ref.at[0], mixers.at[me], own_mix)

    def give_small(by):
        return pltpu.make_async_remote_copy(
            src_ref=smalls.at[me],
            dst_ref=smalls.at[me],
            send_sem=small_send.at[by],
            recv_sem=small_recv.at[me],
            device_id={"span": lax.rem(me + by, n_span)},
            device_id_type=MESH,
        )

    def got_small(g):
        return pltpu.make_async_remote_copy(
            src_ref=smalls.at[g],
            dst_ref=smalls.at[g],
            send_sem=small_send.at[1],
            recv_sem=small_recv.at[g],
            device_id={"span": g},
            device_id_type=MESH,
        )

    def give_mix(r, k, by):
        return pltpu.make_async_remote_copy(
            src_ref=coupling_ref.at[0, r, k, core],
            dst_ref=mixers.at[me, r, k, core],
            send_sem=mix_send.at[r, k, by],
            recv_sem=mix_recv.at[me, r, k],
            device_id={"span": lax.rem(me + by, n_span)},
            device_id_type=MESH,
        )

    def got_mix(g, r, k):
        return pltpu.make_async_remote_copy(
            src_ref=coupling_ref.at[0, r, k, core],
            dst_ref=mixers.at[g, r, k, core],
            send_sem=mix_send.at[r, k, 1],
            recv_sem=mix_recv.at[g, r, k],
            device_id={"span": g},
            device_id_type=MESH,
        )

    def share_mix(g, r, k):
        return pltpu.make_async_remote_copy(
            src_ref=mixers.at[g, r, k, core],
            dst_ref=mixers.at[g, r, k, core],
            send_sem=share_send.at[g, r, k],
            recv_sem=share_recv.at[g, r, k],
            device_id={"tm": sibling},
            device_id_type=MESH,
        )

    def shared_mix(g, r, k):
        return pltpu.make_async_remote_copy(
            src_ref=mixers.at[g, r, k, 1 - core],
            dst_ref=mixers.at[g, r, k, 1 - core],
            send_sem=share_send.at[g, r, k],
            recv_sem=share_recv.at[g, r, k],
            device_id={"tm": sibling},
            device_id_type=MESH,
        )

    def give(t):
        r = t % spans

        @pl.when(t // spans == me)
        def _():
            for k in range(steps):
                for by in range(1, n_span):
                    give_mix(r, k, by).start()

    def relay(t):
        g = t // spans
        r = t % spans

        @pl.when(g != me)
        def _():
            for k in range(steps):
                got_mix(g, r, k).wait_recv()
                share_mix(g, r, k).start()

    def go_up(t, f):
        return pltpu.make_async_remote_copy(
            src_ref=own.at[t, f, :, pl.ds(samples - edge, edge)],
            dst_ref=low_halo.at[t, f],
            send_sem=up_send.at[t, f],
            recv_sem=up_recv.at[t, f],
            device_id={"tm": above},
            device_id_type=MESH,
        )

    def go_down(t, f):
        return pltpu.make_async_remote_copy(
            src_ref=own.at[t, f, :, pl.ds(0, edge)],
            dst_ref=high_halo.at[t, f],
            send_sem=down_send.at[t, f],
            recv_sem=down_recv.at[t, f],
            device_id={"tm": below},
            device_id_type=MESH,
        )

    def send_edges(t, f):
        @pl.when(has_above)
        def _():
            go_up(t, f).start()

        @pl.when(has_below)
        def _():
            go_down(t, f).start()

    def keep_out(g, f):
        return pltpu.make_async_copy(
            ostage.at[g, f], out_ref.at[0, me * per + f], out_send.at[g, f]
        )

    def send_out(g, f):
        return pltpu.make_async_remote_copy(
            src_ref=ostage.at[g, f],
            dst_ref=out_ref.at[0, me * per + f],
            send_sem=out_send.at[g, f],
            recv_sem=out_recv.at[me, f],
            device_id={"span": g},
            device_id_type=MESH,
        )

    def got_out(source, f):
        return pltpu.make_async_remote_copy(
            src_ref=ostage.at[0, f],
            dst_ref=out_ref.at[0, source * per + f],
            send_sem=out_send.at[0, f],
            recv_sem=out_recv.at[source, f],
            device_id={"span": source},
            device_id_type=MESH,
        )

    for f in range(per):
        load(f).start()
    for copy in small_loads:
        copy.start()
    own_mixers.start()

    barrier = pltpu.get_barrier_semaphore()
    for by in range(1, n_span):
        pl.semaphore_signal(
            barrier, inc=1, device_id={"span": lax.rem(me + by, n_span)}, device_id_type=MESH
        )

    @pl.when(has_above)
    def _():
        pl.semaphore_signal(barrier, inc=1, device_id={"tm": above}, device_id_type=MESH)

    @pl.when(has_below)
    def _():
        pl.semaphore_signal(barrier, inc=1, device_id={"tm": below}, device_id_type=MESH)

    for f in range(per):
        load(f).wait()
        for part in range(2):
            own[0, f, pl.ds(part * rows + rows - 8, 8), :] = jnp.zeros((8, samples), jnp.float32)
            own[0, f, pl.ds(part * rows, channels), :] = lstage[f, part]

    square[...] = jnp.zeros(square.shape, jnp.float32)
    for copy in small_loads:
        copy.wait()
    smalls[me] = jnp.zeros(smalls.shape[1:], jnp.float32)
    for r in range(spans):
        for k in range(steps):
            first = 2 * (r * steps + k)
            smalls[me, pl.ds(first, 2), : taps_stage.shape[-1]] = taps_stage[r, k]
    row = lax.broadcasted_iota(jnp.int32, (2 * LANES, 2 * LANES), 0)
    column = lax.broadcasted_iota(jnp.int32, (2 * LANES, 2 * LANES), 1)
    turned = jnp.where((row + column == 0) | (row + column == 2 * LANES), 1.0, 0.0)
    smalls[me, :gain_row] = jnp.dot(
        smalls[me, :gain_row],
        turned,
        precision=lax.Precision.HIGHEST,
        preferred_element_type=jnp.float32,
    )
    smalls[me, pl.ds(gain_row, spans), :channels] = gain_stage[...]
    smalls[me, pl.ds(rate_row, spans), :steps] = rate_stage[...]

    pl.semaphore_wait(
        barrier,
        n_span - 1 + jnp.where(has_above, 1, 0) + jnp.where(has_below, 1, 0),
    )
    give(0)
    for f in range(per):
        send_edges(0, f)
    for by in range(1, n_span):
        give_small(by).start()
    own_mixers.wait()

    def chosen(g, r, first):
        both = smalls[g, pl.ds(first, spans)]
        return jnp.sum(
            jnp.where(lax.broadcasted_iota(jnp.int32, both.shape, 0) == r, both, 0.0),
            axis=0,
            keepdims=True,
        )

    def prepare(t):
        g = t // spans
        r = t % spans

        @pl.when((g != me) & (r == 0))
        def _():
            got_small(g).wait_recv()

        for k in range(steps):

            @pl.when(g != me)
            def _():
                shared_mix(g, r, k).wait_recv()

            real = mixers[g, r, k, 0]
            imag = mixers[g, r, k, 1]
            square[:channels, :channels] = real
            square[:channels, pl.ds(LANES, channels)] = -imag
            square[pl.ds(rows, channels), :channels] = imag
            square[pl.ds(rows, channels), pl.ds(LANES, channels)] = real
            high, low = halves(square[...])
            mix[0, k] = high
            mix[1, k] = low
            pair = smalls[g, pl.ds(0, gain_row)]
            which = lax.broadcasted_iota(jnp.int32, pair.shape, 0)
            for part in range(2):
                line = jnp.sum(
                    jnp.where(which == 2 * (r * steps + k) + part, pair, 0.0),
                    axis=0,
                    keepdims=True,
                )
                line = jnp.broadcast_to(line, (LANES, 2 * LANES))
                band = pltpu.roll(line, 0, 1, stride=1, stride_axis=0)
                column = pl.ds(part * LANES, LANES)
                high, low = halves(band)
                for half in range(2):
                    place = pl.ds(half * LANES, LANES)
                    fir[0, k, place, column] = high[:, half * LANES : (half + 1) * LANES]
                    fir[1, k, place, column] = low[:, half * LANES : (half + 1) * LANES]

    gap = jnp.zeros((LANES - rows, 1), jnp.bfloat16)

    def spread(real, imag):
        fill = jnp.broadcast_to(gap, (LANES - rows, real.shape[1]))
        return jnp.concatenate([real, fill, imag, fill], axis=0)

    def advance(t, f):
        g = t // spans
        r = t % spans
        blocks = (
            [low_halo[t, f, :, pl.ds(i, LANES)] for i in range(0, edge, LANES)]
            + [own[t, f, :, pl.ds(i, LANES)] for i in range(0, samples, LANES)]
            + [high_halo[t, f, :, pl.ds(i, LANES)] for i in range(0, edge, LANES)]
        )
        rates = chosen(g, r, rate_row)
        gain = chosen(g, r, gain_row)[:, :LANES]
        gain = jnp.broadcast_to(gain, (LANES, LANES)).T[:rows]
        gain = jnp.concatenate([gain] * (samples // LANES), axis=1)
        margin = edge
        for k in range(steps):
            margin = margin - edge // steps
            split = [halves(block) for block in blocks]
            count = len(blocks) - 1
            real_parts = []
            imag_parts = []
            for b in range(count):
                wide = product(
                    jnp.concatenate([split[b][0], split[b + 1][0]], axis=1),
                    jnp.concatenate([split[b][1], split[b + 1][1]], axis=1),
                    fir[0, k],
                    fir[1, k],
                )
                real_parts.append(wide[:rows, :LANES] - wide[rows:, LANES:])
                imag_parts.append(wide[:rows, LANES:] + wide[rows:, :LANES])
            real = jnp.concatenate(real_parts, axis=1)
            imag = jnp.concatenate(imag_parts, axis=1)
            if margin > 0:
                extent = count * LANES
                place = tm * samples - margin + lax.broadcasted_iota(jnp.int32, (1, extent), 1)
                inside = ((place >= 0) & (place < samples * n_tm)).astype(jnp.float32)
                real = real * inside
                imag = imag * inside
            real_high, real_low = halves(real)
            imag_high, imag_low = halves(imag)
            mixed = product(
                mix[0, k],
                mix[1, k],
                spread(real_high, imag_high),
                spread(real_low, imag_low),
            )
            power = jnp.sum(mixed * mixed, axis=0, keepdims=True)
            cosine, sine = cos_sin(power * rates[:, k : k + 1])
            real = mixed[:rows] * cosine - mixed[rows:] * sine
            imag = mixed[:rows] * sine + mixed[rows:] * cosine
            if k == steps - 1:
                real = real * gain
                imag = imag * gain
            both = jnp.concatenate([real, imag], axis=0)
            blocks = [both[:, b * LANES : (b + 1) * LANES] for b in range(count)]
        own[t + 1, f] = both

        @pl.when(t + 1 < rounds)
        def _():
            send_edges(t + 1, f)

        @pl.when(r == spans - 1)
        def _():
            ostage[g, f, 0] = real[:channels]
            ostage[g, f, 1] = imag[:channels]

            @pl.when(g == me)
            def _():
                keep_out(g, f).start()

            @pl.when(g != me)
            def _():
                send_out(g, f).start()

    relay(0)
    prepare(0)
    for t in range(1, rounds):
        give(t)

    def one_round(t, carry):
        for f in range(per):

            @pl.when(has_below)
            def _():
                go_up(t, f).wait_recv()

            @pl.when(jnp.logical_not(has_below))
            def _():
                low_halo[t, f] = jnp.zeros(low_halo.shape[2:], jnp.float32)

            @pl.when(has_above)
            def _():
                go_down(t, f).wait_recv()

            @pl.when(jnp.logical_not(has_above))
            def _():
                high_halo[t, f] = jnp.zeros(high_halo.shape[2:], jnp.float32)

            advance(t, f)
            if f == 0:

                @pl.when(t + 1 < rounds)
                def _():
                    relay(t + 1)

        @pl.when(t + 1 < rounds)
        def _():
            prepare(t + 1)

        return carry

    lax.fori_loop(0, rounds, one_round, 0)

    def drain(t, carry):
        for f in range(per):

            @pl.when(has_above)
            def _():
                go_up(t, f).wait_send()

            @pl.when(has_below)
            def _():
                go_down(t, f).wait_send()

        return carry

    lax.fori_loop(0, rounds, drain, 0)
    for by in range(1, n_span):
        give_small(by).wait_send()
        for r in range(spans):
            for k in range(steps):
                give_mix(r, k, by).wait_send()

    def drain_shares(t, carry):
        @pl.when(t // spans != me)
        def _():
            for k in range(steps):
                share_mix(t // spans, t % spans, k).wait_send()

        return carry

    lax.fori_loop(0, rounds, drain_shares, 0)

    def finish(g, carry):
        for f in range(per):

            @pl.when(g == me)
            def _():
                keep_out(g, f).wait()

            @pl.when(g != me)
            def _():
                send_out(g, f).wait_send()
                got_out(g, f).wait_recv()

        return carry

    lax.fori_loop(0, n_span, finish, 0)


def shards(launched, coupling, impulse, amplifier, nonlinear):
    n_span = lax.axis_size("span")
    n_tm = lax.axis_size("tm")
    frames, _, channels, samples = launched.shape
    _, spans, steps, _, taps = impulse.shape
    per = frames // n_span
    rows = padded_rows(channels)
    edge = steps * (taps - 1) // 2
    rounds = n_span * spans
    small_rows = (2 * spans * steps + 2 * spans + 7) // 8 * 8
    sizes = (n_span, n_tm, spans, steps, channels, samples, per, edge)
    mine = lax.dynamic_slice_in_dim(launched, lax.axis_index("span") * per, per, 0)
    dma = pltpu.SemaphoreType.DMA
    return pl.pallas_call(
        functools.partial(kernel, sizes),
        out_shape=jax.ShapeDtypeStruct((1,) + launched.shape, jnp.float32),
        in_specs=[pl.BlockSpec(memory_space=pl.ANY)] * 5,
        out_specs=pl.BlockSpec(memory_space=pl.ANY),
        scratch_shapes=[
            pltpu.VMEM((per, 2, channels, samples), jnp.float32),
            pltpu.VMEM(impulse.shape[1:], jnp.float32),
            pltpu.VMEM(amplifier.shape[1:], jnp.float32),
            pltpu.VMEM(nonlinear.shape[1:], jnp.float32),
            pltpu.VMEM((rounds + 1, per, 2 * rows, samples), jnp.float32),
            pltpu.VMEM((rounds, per, 2 * rows, edge), jnp.float32),
            pltpu.VMEM((rounds, per, 2 * rows, edge), jnp.float32),
            pltpu.VMEM((n_span,) + coupling.shape[1:], jnp.float32),
            pltpu.VMEM((n_span, small_rows, 2 * LANES), jnp.float32),
            pltpu.VMEM((2 * rows, 2 * LANES), jnp.float32),
            pltpu.VMEM((2, steps, 2 * rows, 2 * LANES), jnp.bfloat16),
            pltpu.VMEM((2, steps, 2 * LANES, 2 * LANES), jnp.bfloat16),
            pltpu.VMEM((n_span, per, 2, channels, samples), jnp.float32),
            dma((per,)),
            dma((3,)),
            dma,
            dma((n_span,)),
            dma((n_span,)),
            dma((spans, steps, n_span)),
            dma((n_span, spans, steps)),
            dma((n_span, spans, steps)),
            dma((n_span, spans, steps)),
            dma((rounds, per)),
            dma((rounds, per)),
            dma((rounds, per)),
            dma((rounds, per)),
            dma((n_span, per)),
            dma((n_span, per)),
        ],
        compiler_params=pltpu.CompilerParams(
            collective_id=0, has_side_effects=True, vmem_limit_bytes=48 * 1024 * 1024
        ),
        name="link",
    )(mine, coupling, impulse, amplifier, nonlinear)


def solution(mesh):
    placed = (
        P(None, None, None, "tm"),
        P("span", None, None, None, None, None),
        P("span", None, None, None, None),
        P("span", None, None),
        P("span", None, None),
    )
    return jax.shard_map(
        shards,
        mesh=mesh,
        in_specs=placed,
        out_specs=P("span", None, None, None, "tm"),
        check_vma=False,
    )
```
